32 devices in a mesh: rows: 8 (over y, x, core), cols: 4 (over z).
Axes of the slice: x: 2, y: 2, z: 4, core: 2. Of those that a mesh axis runs over, the one named last changes fastest.
Arguments:
- vectors: float32 [128, 81920], P('cols', 'rows'), may hold values from -6 to 6
- directions: float32 [128, 81920], P('cols', 'rows'), may hold values from -6 to 6
- tables: float32 [4, 640, 640], replicated, may hold values from -1 to 3
- counts: int32 [8], P('rows'), may hold values from 8 to 16, as said below
- send_lists: int32 [8, 2, 3], P('rows'), may hold values from 0 to 15, as said below
- neighbors: int32 [128, 7], P('rows'), may hold values from 0 to 21
- coupling_kinds: int32 [128, 7], P('rows'), may hold values from 0 to 3
- rotations: float32 [2, 384, 256], replicated, may hold values from -0.3125 to 0.3125
Outputs:
- new_vectors: float32 [128, 81920], P('cols', 'rows')
- new_directions: float32 [128, 81920], P('cols', 'rows')
The draws below stay inside these ranges and needn't reach their ends.
Inputs may be any that keep to these rules, and one draw needn't show every extreme that they name: `counts`: at least one index of rows holds 16 live slots. `send_lists`: each list names 3 different live slots of its own index.
All inputs are finite; a program needn't handle non-finite values.
Results may differ from the reference program's by a relative error of at most 0.0003.
Values sent between devices are 32-bit elements; how exact they have to be, the bound alone decides.
A program may use at most 128 MiB of HBM per device.

```python
import math
import jax
import jax.numpy as jnp
from jax import lax

B = 640
K = 128
CAP = 16
GHOST = 3
NB = 7
TYPES = 4
ITERS = 2
SLOTS = 128
ROWS_ALL = 81920
N_ROWS = 8


def live_counts(key):
    raw_counts = jax.random.randint(key, (N_ROWS,), CAP // 2, CAP + 1)
    full_index = jax.random.randint(jax.random.fold_in(key, 1), (), 0, N_ROWS)
    return jnp.where(jnp.arange(N_ROWS) == full_index, CAP, raw_counts).astype(jnp.int32)


def draw_counts(key, part):
    return live_counts(key)


def draw_send_lists(key, part):
    counts = live_counts(key)
    key = jax.random.fold_in(key, 7)
    slot_ids = jnp.arange(CAP, dtype=jnp.int32)
    scores = jax.random.randint(key, (N_ROWS, 2, CAP), 0, 1 << 20) * CAP + slot_ids
    scores = jnp.where(slot_ids[None, None, :] < counts[:, None, None], scores, 1 << 30)
    ordering = jnp.argsort(scores, axis=-1)
    return ordering[:, :, :GHOST].astype(jnp.int32)


def draw_tables(key, part):
    key = jax.random.fold_in(key, 11)
    noise_key = jax.random.fold_in(key, 1)
    level_key = jax.random.fold_in(key, 2)
    spread = (B * NB) ** (-0.5)
    noise = jnp.clip(jax.random.normal(noise_key, (TYPES, B, B), jnp.float32), -6.0, 6.0) * spread
    levels = jnp.exp(jax.random.uniform(level_key, (TYPES,), jnp.float32, math.log(0.5), math.log(2.0)))
    onsite = levels[:, None, None] * jnp.eye(B, dtype=jnp.float32)[None, :, :]
    return noise + onsite


def place_ends(drawn, key, least, high):
    place = [jax.random.randint(jax.random.fold_in(key, axis), (), 0, length) for axis, length in enumerate(drawn.shape)]
    widest = drawn.shape.index(max(drawn.shape))
    beside = place[:widest] + [(place[widest] + 1) % drawn.shape[widest]] + place[widest + 1:]
    return drawn.at[tuple(place)].set(least).at[tuple(beside)].set(high)


def steps_of(key, dims, pieces, least, largest):
    factor_of, own = 1.0, jax.random.fold_in(key, 6)
    for dim, parts in pieces:
        steps = jnp.exp(jax.random.uniform(jax.random.fold_in(own, dim), (parts,), jnp.float32, least / len(pieces), largest / len(pieces)))
        factor_of = factor_of * jnp.repeat(steps, dims[dim] // parts).reshape([-1 if axis == dim else 1 for axis in range(len(dims))])
    return factor_of


def scatter_about(key, extent, width, most, shards=(), held_as=jnp.bfloat16):
    drawn = width * jax.random.normal(key, extent, jnp.float32)
    if shards:
        drawn = drawn * steps_of(key, extent, shards, -0.22, 0.18)
    return jnp.clip(drawn, -most, most).astype(held_as)


def setup_inputs(seed: int = 0) -> dict:
    keys = jax.random.split(jax.random.key(seed), 9)
    vectors = scatter_about(keys[0], (K, ROWS_ALL), 1.0, 6.0, ((0, 4), (1, 8)), jnp.float32)
    directions = scatter_about(keys[1], (K, ROWS_ALL), 1.0, 6.0, ((0, 4), (1, 8)), jnp.float32)
    tables = draw_tables(jax.random.fold_in(keys[8], 71), 0)
    counts = draw_counts(jax.random.fold_in(keys[8], 71), 0)
    send_lists = draw_send_lists(jax.random.fold_in(keys[8], 71), 0)
    neighbors = place_ends(jax.random.randint(keys[5], (SLOTS, NB), 0, CAP + 2 * GHOST), jax.random.fold_in(keys[5], 1), 0, (CAP + 2 * GHOST) - 1).astype(jnp.int32)
    coupling_kinds = place_ends(jax.random.randint(keys[6], (SLOTS, NB), 0, TYPES), jax.random.fold_in(keys[6], 1), 0, TYPES - 1).astype(jnp.int32)
    rotations = scatter_about(keys[7], (ITERS, 3 * K, 2 * K), (3 * K) ** -0.5, 0.3125, (), jnp.float32)
    return dict(vectors=vectors, directions=directions, tables=tables, counts=counts, send_lists=send_lists, neighbors=neighbors, coupling_kinds=coupling_kinds, rotations=rotations)


highest = lax.Precision.HIGHEST

def apply_hamiltonian(vectors, tables, send_lists, neighbors, coupling_kinds):
    col_count = vectors.shape[0]
    blocks = vectors.reshape(col_count, N_ROWS, CAP, B).transpose(1, 2, 0, 3)
    upward = jax.vmap(lambda blk_set, index_set: blk_set[index_set])(blocks, send_lists[:, 1])
    downward = jax.vmap(lambda blk_set, index_set: blk_set[index_set])(blocks, send_lists[:, 0])
    nothing = jnp.zeros_like(upward[:1])
    lower_ghosts = jnp.concatenate([nothing, upward[:-1]], axis=0)
    upper_ghosts = jnp.concatenate([downward[1:], nothing], axis=0)
    extended = jnp.concatenate([lower_ghosts, blocks, upper_ghosts], axis=1)
    near_ids = neighbors.reshape(N_ROWS, CAP, NB)
    near_kinds = coupling_kinds.reshape(N_ROWS, CAP, NB)

    def one_device(packed):
        ext_blocks, ids_here, kinds_here = packed
        picked = ext_blocks[ids_here]
        onehot = (kinds_here[:, :, None] == jnp.arange(TYPES, dtype=jnp.int32)).astype(jnp.float32)
        grouped = jnp.einsum('cnt,cnkb->tckb', onehot, picked, precision=highest)
        return jnp.einsum('tckb,tbe->cke', grouped, tables, precision=highest)
    result = lax.map(one_device, (extended, near_ids, near_kinds))
    return result.transpose(2, 0, 1, 3).reshape(col_count, N_ROWS * CAP * B)

def reference(vectors, directions, tables, counts, send_lists, neighbors, coupling_kinds, rotations):
    live_slots = (jnp.arange(CAP, dtype=jnp.int32)[None, :] < counts[:, None]).astype(jnp.float32)
    row_mask = jnp.repeat(live_slots.reshape(-1), B)
    row_total = float(N_ROWS * CAP * B)
    current = vectors * row_mask
    previous = directions * row_mask
    for iteration in range(ITERS):
        applied = apply_hamiltonian(current, tables, send_lists, neighbors, coupling_kinds) * row_mask
        rayleigh = jnp.dot(applied, current.T, precision=highest) / row_total
        residual = applied - jnp.dot(rayleigh, current, precision=highest)
        stacked = jnp.concatenate([residual, current, previous], axis=0)
        gram_matrix = jnp.dot(stacked, stacked.T, precision=highest) / row_total
        factor = jnp.linalg.cholesky(gram_matrix)
        solved = lax.linalg.triangular_solve(factor, rotations[iteration], left_side=True, lower=True, transpose_a=True)
        current = jnp.dot(solved[:, :K].T, stacked, precision=highest)
        previous = jnp.dot(solved[:, K:].T, stacked, precision=highest)
    return (current, previous)
```

```python
import functools
import jax
import jax.numpy as jnp
from jax import lax
from jax.experimental import pallas as pl
from jax.experimental.pallas import tpu as pltpu
from jax.sharding import PartitionSpec as P

highest = lax.Precision.HIGHEST
high = lax.Precision.HIGH
AXES = ("rows", "cols")


def shifted(array, axis, by):
    devices = lax.axis_size(axis)
    pairs = [(i, i + by) for i in range(devices) if 0 <= i + by < devices]
    return lax.ppermute(array, axis, pairs)


def split_parts(array):
    top = lax.reduce_precision(array, 8, 7)
    return top.astype(jnp.bfloat16), (array - top).astype(jnp.bfloat16)


def hamiltonian_kernel(group, counts, near, kinds, ext, top_ref, low_ref, out_ref, sums):
    types, depth, cols = sums.shape[0], sums.shape[2], out_ref.shape[1]
    step = pl.program_id(0)
    sums[...] = jnp.zeros_like(sums)
    for s in range(group):
        slot = step * group + s
        for j in range(near.shape[1]):
            where = kinds[slot, j]
            rows = pl.ds(s * cols, cols)
            sums[where, rows, :] = sums[where, rows, :] + ext[near[slot, j]]
    total = jnp.zeros((group * cols, depth), jnp.float32)
    for t in range(types):
        value = sums[t]
        top = value.astype(jnp.bfloat16)
        low = (value - top.astype(jnp.float32)).astype(jnp.bfloat16)
        dot = functools.partial(jnp.dot, preferred_element_type=jnp.float32)
        total += dot(top, top_ref[t]) + (dot(low, top_ref[t]) + dot(top, low_ref[t]))
    for s in range(group):
        live = ((step * group + s) < counts[0]).astype(jnp.float32)
        out_ref[s] = total[s * cols : (s + 1) * cols] * live


def apply_hamiltonian(blocks, tables_top, tables_low, counts, send_lists, neighbors, kinds):
    slots, cols, depth = blocks.shape
    types = tables_top.shape[0]
    lower = shifted(blocks[send_lists[0, 1]], "rows", 1)
    upper = shifted(blocks[send_lists[0, 0]], "rows", -1)
    extended = jnp.concatenate([lower, blocks, upper], axis=0)
    group = 4
    whole = lambda shape: pl.BlockSpec(shape, lambda i: (0,) * len(shape))
    smem = pl.BlockSpec(memory_space=pltpu.SMEM)
    return pl.pallas_call(
        functools.partial(hamiltonian_kernel, group),
        grid=(slots // group,),
        out_shape=jax.ShapeDtypeStruct(blocks.shape, jnp.float32),
        in_specs=[
            smem,
            smem,
            smem,
            whole(extended.shape),
            whole(tables_top.shape),
            whole(tables_low.shape),
        ],
        out_specs=pl.BlockSpec((group, cols, depth), lambda i: (i, 0, 0)),
        scratch_shapes=[pltpu.VMEM((types, group * cols, depth), jnp.float32)],
        compiler_params=pltpu.CompilerParams(vmem_limit_bytes=48 * 2**20),
        cost_estimate=pl.CostEstimate(
            flops=6 * types * slots * cols * depth * depth,
            bytes_accessed=4 * (extended.size + tables_top.size + blocks.size),
            transcendentals=0,
        ),
    )(counts, neighbors, kinds, extended, tables_top, tables_low)


def dot_nn(a, b):
    return jnp.dot(a, b, precision=highest, preferred_element_type=jnp.float32)


def dot_nt(a, b):
    return lax.dot_general(
        a, b, (((1,), (1,)), ((), ())), precision=highest, preferred_element_type=jnp.float32
    )


def dot_tn(a, b):
    return lax.dot_general(
        a, b, (((0,), (0,)), ((), ())), precision=highest, preferred_element_type=jnp.float32
    )


def inverse_factor(a):
    n = a.shape[0]
    ids = lax.broadcasted_iota(jnp.int32, (n, n), 0)
    lanes = lax.broadcasted_iota(jnp.int32, (n, n), 1)
    row_ids = lax.broadcasted_iota(jnp.int32, (n, 1), 0)
    eye = (ids == lanes).astype(jnp.float32)
    a_rows = [a[r : r + 8] for r in range(0, n, 8)]
    i_rows = [eye[r : r + 8] for r in range(0, n, 8)]
    for k in range(n - 1):
        g, r = k // 8, k % 8
        row_a, row_i = a_rows[g][r : r + 1], i_rows[g][r : r + 1]
        inv = 1.0 / row_a[:, k : k + 1]
        row_a, row_i = row_a * inv, row_i * inv
        for h in range(g, n // 8):
            factor = a_rows[h][:, k : k + 1]
            if h == g:
                factor = jnp.where(row_ids[g * 8 : g * 8 + 8] > k, factor, 0.0)
            a_rows[h] = a_rows[h] - factor * row_a
            i_rows[h] = i_rows[h] - factor * row_i
    a = jnp.concatenate(a_rows, axis=0)
    inverse = jnp.concatenate(i_rows, axis=0)
    pivots = jnp.sum(jnp.where(ids == lanes, a, 0.0), axis=1, keepdims=True)
    return inverse * lax.rsqrt(pivots)


def chain_kernel(gram_ref, rot_ref, out_ref, work, inv_ref, coef, mixed):
    k = gram_ref.shape[0] // 5
    at = lambda i: slice(i * k, (i + 1) * k)
    three = work.shape[0] // k

    def solve(iteration):
        rayleigh = work[at(0), at(1)]
        changed = work[at(0), :] - dot_nn(rayleigh, work[at(1), :])
        corner = changed[:, at(0)] - dot_nt(changed[:, at(1)], rayleigh)
        work[at(0), at(0)] = corner
        for i in (1, 2):
            work[at(i), at(0)] = changed[:, at(i)].T

        def block(b, carry):
            here = pl.ds(pl.multiple_of(b * k, k), k)
            inv_ref[here, :] = inverse_factor(work[here, here])
            return carry

        for b in range(three):
            block(b, 0)
            inverse = inv_ref[at(b), :]
            panels = [dot_nt(work[at(i), at(b)], inverse) for i in range(b + 1, three)]
            for i in range(b + 1, three):
                work[at(i), at(b)] = panels[i - b - 1]
                for j in range(b + 1, i + 1):
                    work[at(i), at(j)] = work[at(i), at(j)] - dot_nt(
                        panels[i - b - 1], panels[j - b - 1]
                    )
        parts = [None] * three
        for b in reversed(range(three)):
            value = rot_ref[iteration, at(b), :]
            for i in range(b + 1, three):
                value = value - dot_tn(work[at(i), at(b)], parts[i])
            parts[b] = dot_tn(inv_ref[at(b), :], value)
        coef[at(0), :] = parts[0]
        coef[at(1), :] = parts[1] - dot_tn(rayleigh, parts[0])
        coef[at(2), :] = parts[2]

    order = (2, 0, 1)
    for i in range(3):
        for j in range(3):
            work[at(i), at(j)] = gram_ref[at(order[i]), at(order[j])]
    solve(0)
    mixed[...] = jnp.zeros_like(mixed)
    for source, plain, applied in ((0, 2, 4), (1, 0, 2), (2, 1, 3)):
        first = coef[at(source), at(0)]
        mixed[at(applied), at(0)] = first
        mixed[at(plain), at(1)] = first
        mixed[at(plain), at(2)] = coef[at(source), at(1)]
    work[...] = dot_tn(mixed[...], dot_nn(gram_ref[...], mixed[...]))
    solve(1)
    out_ref[...] = dot_nn(mixed[...], coef[...])


def rotation_chain(gram, rotations):
    size = gram.shape[0]
    k = size // 5
    return pl.pallas_call(
        chain_kernel,
        out_shape=jax.ShapeDtypeStruct((size, 2 * k), jnp.float32),
        in_specs=[pl.BlockSpec(memory_space=pltpu.VMEM)] * 2,
        out_specs=pl.BlockSpec(memory_space=pltpu.VMEM),
        scratch_shapes=[
            pltpu.VMEM((3 * k, 3 * k), jnp.float32),
            pltpu.VMEM((3 * k, k), jnp.float32),
            pltpu.VMEM((3 * k, 2 * k), jnp.float32),
            pltpu.VMEM((size, 3 * k), jnp.float32),
        ],
        compiler_params=pltpu.CompilerParams(vmem_limit_bytes=48 * 2**20),
    )(gram, rotations)


def summed(values):
    rows, cols = lax.axis_size("rows"), lax.axis_size("cols")
    shape = values.shape
    swap = functools.partial(lax.all_to_all, split_axis=0, concat_axis=0, tiled=True)
    parts = values.reshape(rows, cols, -1)
    part = jnp.sum(swap(parts, "rows"), axis=0)
    part = jnp.sum(swap(part, "cols"), axis=0)
    line = swap(jnp.broadcast_to(part, (cols,) + part.shape), "cols")
    return swap(jnp.broadcast_to(line, (rows,) + line.shape), "rows").reshape(shape)


def on_device(
    vectors, directions, tables, counts, send_lists, neighbors, coupling_kinds, rotations
):
    local, length = vectors.shape
    slots = neighbors.shape[0]
    depth = length // slots
    cols = lax.axis_size("cols")
    k = local * cols
    row_total = float(length * lax.axis_size("rows"))
    live = (jnp.arange(slots, dtype=jnp.int32) < counts[0]).astype(jnp.float32)
    both = jnp.concatenate([vectors, directions], axis=0).reshape(2 * local, slots, depth)
    both = both.transpose(1, 0, 2) * live[:, None, None]
    top, low = split_parts(tables)
    apply = functools.partial(
        apply_hamiltonian,
        tables_top=top,
        tables_low=low,
        counts=counts,
        send_lists=send_lists,
        neighbors=neighbors,
        kinds=coupling_kinds,
    )

    def to_rows(blocks):
        swapped = lax.all_to_all(blocks, "cols", split_axis=0, concat_axis=0, tiled=True)
        count = blocks.shape[1] // local
        swapped = swapped.reshape(cols, slots // cols, count, local, depth)
        return swapped.transpose(2, 0, 3, 1, 4).reshape(count * k, length // cols)

    both_rows = to_rows(both)
    applied = apply(both)
    applied_rows = to_rows(applied)
    twice = apply(applied[:, :local])
    basis = jnp.concatenate([both_rows, applied_rows, to_rows(twice)], axis=0)
    gram = jnp.dot(basis, basis.T, precision=high)
    pairs = [(i, j) for i in range(5) for j in range(i + 1)]
    at = lambda i: slice(i * k, (i + 1) * k)
    packed = summed(jnp.concatenate([gram[at(i), at(j)] for i, j in pairs], axis=0)) / row_total
    tiles = {pair: packed[at(n)] for n, pair in enumerate(pairs)}
    gram = jnp.concatenate(
        [
            jnp.concatenate(
                [tiles[i, j] if i >= j else tiles[j, i].T for j in range(5)], axis=1
            )
            for i in range(5)
        ],
        axis=0,
    )
    mix = rotation_chain(gram, rotations)

    def finish(part):
        made = lax.dot_general(part, basis, (((0,), (0,)), ((), ())), precision=high)
        return lax.all_to_all(made, "cols", split_axis=0, concat_axis=1, tiled=True)

    return (finish(mix[:, :k]), finish(mix[:, k:]))


def solution(mesh):
    return jax.shard_map(
        on_device,
        mesh=mesh,
        in_specs=(
            P("cols", "rows"),
            P("cols", "rows"),
            P(),
            P("rows"),
            P("rows", None, None),
            P("rows", None),
            P("rows", None),
            P(),
        ),
        out_specs=(P("cols", "rows"), P("cols", "rows")),
        check_vma=False,
    )
```

```python
import functools
import jax
import jax.numpy as jnp
from jax import lax
from jax.experimental import pallas as pl
from jax.experimental.pallas import tpu as pltpu
from jax.sharding import PartitionSpec as P

highest = lax.Precision.HIGHEST
high = lax.Precision.HIGH
AXES = ("rows", "cols")


def shifted(array, axis, by):
    devices = lax.axis_size(axis)
    pairs = [(i, i + by) for i in range(devices) if 0 <= i + by < devices]
    return lax.ppermute(array, axis, pairs)


def split_parts(array):
    top = lax.reduce_precision(array, 8, 7)
    return top.astype(jnp.bfloat16), (array - top).astype(jnp.bfloat16)


def hamiltonian_kernel(group, counts, near, kinds, ext, top_ref, low_ref, out_ref, sums):
    types, depth, cols = sums.shape[0], sums.shape[2], out_ref.shape[1]
    step = pl.program_id(0)
    sums[...] = jnp.zeros_like(sums)
    for s in range(group):
        slot = step * group + s
        for j in range(near.shape[1]):
            where = kinds[slot, j]
            rows = pl.ds(s * cols, cols)
            sums[where, rows, :] = sums[where, rows, :] + ext[near[slot, j]]
    total = jnp.zeros((group * cols, depth), jnp.float32)
    for t in range(types):
        value = sums[t]
        top = value.astype(jnp.bfloat16)
        low = (value - top.astype(jnp.float32)).astype(jnp.bfloat16)
        dot = functools.partial(jnp.dot, preferred_element_type=jnp.float32)
        total += dot(top, top_ref[t]) + (dot(low, top_ref[t]) + dot(top, low_ref[t]))
    for s in range(group):
        live = ((step * group + s) < counts[0]).astype(jnp.float32)
        out_ref[s] = total[s * cols : (s + 1) * cols] * live


def apply_hamiltonian(blocks, tables_top, tables_low, counts, send_lists, neighbors, kinds):
    slots, cols, depth = blocks.shape
    types = tables_top.shape[0]
    lower = shifted(blocks[send_lists[0, 1]], "rows", 1)
    upper = shifted(blocks[send_lists[0, 0]], "rows", -1)
    extended = jnp.concatenate([lower, blocks, upper], axis=0)
    group = 4
    whole = lambda shape: pl.BlockSpec(shape, lambda i: (0,) * len(shape))
    smem = pl.BlockSpec(memory_space=pltpu.SMEM)
    return pl.pallas_call(
        functools.partial(hamiltonian_kernel, group),
        grid=(slots // group,),
        out_shape=jax.ShapeDtypeStruct(blocks.shape, jnp.float32),
        in_specs=[
            smem,
            smem,
            smem,
            whole(extended.shape),
            whole(tables_top.shape),
            whole(tables_low.shape),
        ],
        out_specs=pl.BlockSpec((group, cols, depth), lambda i: (i, 0, 0)),
        scratch_shapes=[pltpu.VMEM((types, group * cols, depth), jnp.float32)],
        compiler_params=pltpu.CompilerParams(vmem_limit_bytes=48 * 2**20),
        cost_estimate=pl.CostEstimate(
            flops=6 * types * slots * cols * depth * depth,
            bytes_accessed=4 * (extended.size + tables_top.size + blocks.size),
            transcendentals=0,
        ),
    )(counts, neighbors, kinds, extended, tables_top, tables_low)


def dot_nn(a, b):
    return jnp.dot(a, b, precision=highest, preferred_element_type=jnp.float32)


def dot_nt(a, b):
    return lax.dot_general(
        a, b, (((1,), (1,)), ((), ())), precision=highest, preferred_element_type=jnp.float32
    )


def dot_tn(a, b):
    return lax.dot_general(
        a, b, (((0,), (0,)), ((), ())), precision=highest, preferred_element_type=jnp.float32
    )


def inverse_factor(a):
    n = a.shape[0]
    wide = 8
    ids = lax.broadcasted_iota(jnp.int32, (n, n), 0)
    lanes = lax.broadcasted_iota(jnp.int32, (n, n), 1)
    row_ids = lax.broadcasted_iota(jnp.int32, (wide, n), 0)
    eye = (ids == lanes).astype(jnp.float32)
    a_rows = [a[r : r + wide] for r in range(0, n, wide)]
    i_rows = [eye[r : r + wide] for r in range(0, n, wide)]

    def column(rows, k):
        return jnp.broadcast_to(rows[:, k : k + 1], (wide, n))

    for g in range(n // wide):
        first = g * wide
        pa, pi = a_rows[g], i_rows[g]
        held = [column(pa, first + j) for j in range(wide)]
        inverses, factors = [], []
        for j in range(wide):
            inv = 1.0 / held[j][j : j + 1]
            factor = jnp.where(row_ids > j, held[j] * inv, 0.0)
            pa = pa - factor * pa[j : j + 1]
            pi = pi - factor * pi[j : j + 1]
            for i in range(j + 1, wide):
                held[i] = held[i] - factor * held[i][j : j + 1]
            inverses.append(inv)
            factors.append(factor)
        a_rows[g], i_rows[g] = pa, pi
        if g == n // wide - 1:
            break
        ya, yi = [None] * wide, [None] * wide
        for j in reversed(range(wide)):
            ya[j] = pa[j : j + 1] * inverses[j]
            yi[j] = pi[j : j + 1] * inverses[j]
            for i in reversed(range(j + 1, wide)):
                ya[j] = ya[j] - factors[j][i : i + 1] * ya[i]
                yi[j] = yi[j] - factors[j][i : i + 1] * yi[i]
        for h in range(g + 1, n // wide):
            rest = a_rows[h]
            sum_a, sum_i = rest, i_rows[h]
            for j in range(wide):
                factor = column(rest, first + j)
                sum_a = sum_a - factor * ya[j]
                sum_i = sum_i - factor * yi[j]
            a_rows[h], i_rows[h] = sum_a, sum_i
    a = jnp.concatenate(a_rows, axis=0)
    inverse = jnp.concatenate(i_rows, axis=0)
    pivots = jnp.sum(jnp.where(ids == lanes, a, 0.0), axis=1, keepdims=True)
    return inverse * lax.rsqrt(pivots)


def chain_kernel(gram_ref, rot_ref, out_ref, work, inv_ref, coef, mixed):
    k = gram_ref.shape[0] // 5
    at = lambda i: slice(i * k, (i + 1) * k)
    three = work.shape[0] // k

    def solve(iteration):
        rayleigh = work[at(0), at(1)]
        changed = work[at(0), :] - dot_nn(rayleigh, work[at(1), :])
        corner = changed[:, at(0)] - dot_nt(changed[:, at(1)], rayleigh)
        work[at(0), at(0)] = corner
        for i in (1, 2):
            work[at(i), at(0)] = changed[:, at(i)].T

        def block(b, carry):
            here = pl.ds(pl.multiple_of(b * k, k), k)
            inv_ref[here, :] = inverse_factor(work[here, here])
            return carry

        for b in range(three):
            block(b, 0)
            inverse = inv_ref[at(b), :]
            panels = [dot_nt(work[at(i), at(b)], inverse) for i in range(b + 1, three)]
            for i in range(b + 1, three):
                work[at(i), at(b)] = panels[i - b - 1]
                for j in range(b + 1, i + 1):
                    work[at(i), at(j)] = work[at(i), at(j)] - dot_nt(
                        panels[i - b - 1], panels[j - b - 1]
                    )
        parts = [None] * three
        for b in reversed(range(three)):
            value = rot_ref[iteration, at(b), :]
            for i in range(b + 1, three):
                value = value - dot_tn(work[at(i), at(b)], parts[i])
            parts[b] = dot_tn(inv_ref[at(b), :], value)
        coef[at(0), :] = parts[0]
        coef[at(1), :] = parts[1] - dot_tn(rayleigh, parts[0])
        coef[at(2), :] = parts[2]

    order = (2, 0, 1)
    for i in range(3):
        for j in range(3):
            work[at(i), at(j)] = gram_ref[at(order[i]), at(order[j])]
    solve(0)
    mixed[...] = jnp.zeros_like(mixed)
    for source, plain, applied in ((0, 2, 4), (1, 0, 2), (2, 1, 3)):
        first = coef[at(source), at(0)]
        mixed[at(applied), at(0)] = first
        mixed[at(plain), at(1)] = first
        mixed[at(plain), at(2)] = coef[at(source), at(1)]
    work[...] = dot_tn(mixed[...], dot_nn(gram_ref[...], mixed[...]))
    solve(1)
    out_ref[...] = dot_nn(mixed[...], coef[...])


def rotation_chain(gram, rotations):
    size = gram.shape[0]
    k = size // 5
    return pl.pallas_call(
        chain_kernel,
        out_shape=jax.ShapeDtypeStruct((size, 2 * k), jnp.float32),
        in_specs=[pl.BlockSpec(memory_space=pltpu.VMEM)] * 2,
        out_specs=pl.BlockSpec(memory_space=pltpu.VMEM),
        scratch_shapes=[
            pltpu.VMEM((3 * k, 3 * k), jnp.float32),
            pltpu.VMEM((3 * k, k), jnp.float32),
            pltpu.VMEM((3 * k, 2 * k), jnp.float32),
            pltpu.VMEM((size, 3 * k), jnp.float32),
        ],
        compiler_params=pltpu.CompilerParams(vmem_limit_bytes=48 * 2**20),
    )(gram, rotations)


def summed(values):
    rows, cols = lax.axis_size("rows"), lax.axis_size("cols")
    shape = values.shape
    swap = functools.partial(lax.all_to_all, split_axis=0, concat_axis=0, tiled=True)
    parts = values.reshape(rows, cols, -1)
    part = jnp.sum(swap(parts, "rows"), axis=0)
    part = jnp.sum(swap(part, "cols"), axis=0)
    line = swap(jnp.broadcast_to(part, (cols,) + part.shape), "cols")
    return swap(jnp.broadcast_to(line, (rows,) + line.shape), "rows").reshape(shape)


def on_device(
    vectors, directions, tables, counts, send_lists, neighbors, coupling_kinds, rotations
):
    local, length = vectors.shape
    slots = neighbors.shape[0]
    depth = length // slots
    cols = lax.axis_size("cols")
    k = local * cols
    row_total = float(length * lax.axis_size("rows"))
    live = (jnp.arange(slots, dtype=jnp.int32) < counts[0]).astype(jnp.float32)
    both = jnp.concatenate([vectors, directions], axis=0).reshape(2 * local, slots, depth)
    both = both.transpose(1, 0, 2) * live[:, None, None]
    top, low = split_parts(tables)
    apply = functools.partial(
        apply_hamiltonian,
        tables_top=top,
        tables_low=low,
        counts=counts,
        send_lists=send_lists,
        neighbors=neighbors,
        kinds=coupling_kinds,
    )

    me = lax.axis_index("cols")
    each = slots // cols

    def to_rows(blocks):
        count = blocks.shape[1] // local
        chunks = blocks.reshape((cols, each) + blocks.shape[1:])
        rows = jnp.zeros((count, cols, local, each * depth), jnp.float32)
        for by in range(cols):
            piece = lax.dynamic_index_in_dim(chunks, (me + by) % cols, 0, keepdims=False)
            if by:
                piece = lax.ppermute(piece, "cols", [(i, (i + by) % cols) for i in range(cols)])
            piece = piece.reshape(each, count, local, depth).transpose(1, 2, 0, 3)
            piece = piece.reshape(count, 1, local, each * depth)
            rows = lax.dynamic_update_slice_in_dim(rows, piece, (me - by) % cols, 1)
        return rows.reshape(count * k, each * depth)

    both_rows = to_rows(both)
    applied = apply(both)
    applied_rows = to_rows(applied)
    twice = apply(applied[:, :local])
    basis = jnp.concatenate([both_rows, applied_rows, to_rows(twice)], axis=0)
    gram = jnp.dot(basis, basis.T, precision=high)
    pairs = [(i, j) for i in range(5) for j in range(i + 1)]
    at = lambda i: slice(i * k, (i + 1) * k)
    packed = summed(jnp.concatenate([gram[at(i), at(j)] for i, j in pairs], axis=0)) / row_total
    tiles = {pair: packed[at(n)] for n, pair in enumerate(pairs)}
    gram = jnp.concatenate(
        [
            jnp.concatenate(
                [tiles[i, j] if i >= j else tiles[j, i].T for j in range(5)], axis=1
            )
            for i in range(5)
        ],
        axis=0,
    )
    mix = rotation_chain(gram, rotations)

    def finish(part):
        made = lax.dot_general(part, basis, (((0,), (0,)), ((), ())), precision=high)
        return lax.all_to_all(made, "cols", split_axis=0, concat_axis=1, tiled=True)

    return (finish(mix[:, :k]), finish(mix[:, k:]))


def solution(mesh):
    return jax.shard_map(
        on_device,
        mesh=mesh,
        in_specs=(
            P("cols", "rows"),
            P("cols", "rows"),
            P(),
            P("rows"),
            P("rows", None, None),
            P("rows", None),
            P("rows", None),
            P(),
        ),
        out_specs=(P("cols", "rows"), P("cols", "rows")),
        check_vma=False,
    )
```
